32 devices in a mesh: dp: 4 (over y, x), expert: 8 (over z, core).
Axes of the slice: x: 2, y: 2, z: 4, core: 2. Of those that a mesh axis runs over, the one named last changes fastest.
Arguments:
- stream: bfloat16 [4096, 7168], P(('dp', 'expert')), may hold values from -30 to 30
- heads_out: bfloat16 [4096, 16384], P(('dp', 'expert')), may hold values from -6 to 6
- cotangent: bfloat16 [4096, 7168], P(('dp', 'expert')), may hold values from -6 to 6
- adapter_down: bfloat16 [16, 16384], replicated, may hold values from -0.046875 to 0.046875
- adapter_raise_factor: bfloat16 [16, 7168], replicated, may hold values from -0.59765625 to 0.59765625
- norm_gain: float32 [7168], replicated, may hold values from 0.5 to 2
- router: bfloat16 [256, 7168], replicated, may hold values from -0.125 to 0.125
- expert_ids: int32 [4096, 8], P(('dp', 'expert')), may hold values from 0 to 255, as said below
- w_gate_up: bfloat16 [8, 7168, 2, 1024], P('expert', None, None, 'dp'), may hold values from -0.0625 to 0.0625
- w_down: bfloat16 [8, 1024, 7168], P('expert', 'dp'), may hold values from -0.1875 to 0.1875
Outputs:
- residual_stream_gradient: bfloat16 [4096, 7168], P(('dp', 'expert'))
- grad_down: float32 [16, 16384], replicated
- raise_factor_gradient: float32 [16, 7168], replicated
The draws below stay inside these ranges and needn't reach their ends.
Inputs may be any that keep to these rules, and one draw needn't show every extreme that they name: `expert_ids`: each row names 8 different experts. Within each aligned block of 128 rows (the tokens of one device) every expert below 8 is named by at most 6 rows, and one of them is named by exactly 6 rows in every block; the order of a row's ids carries no meaning.
All inputs are finite; a program needn't handle non-finite values.
Results may differ from the reference program's by a relative error of at most 0.0085.
Values may be sent and summed in bfloat16 or wider, within the bound.
A program may use at most 192 MiB of HBM per device.

```python
import jax
import jax.numpy as jnp
from jax import lax

D = 7168
HV = 16384
RANK = 16
ALL_EXP = 256
TOPK = 8
HID = 1024
T_DEV = 128
TOKENS = 4096
WIN = 8
CAP = 6
N_DP = 4
N_EXPERT = 8


def draw_stream(key, part):
    key_base, key_rows, key_cols = jax.random.split(key, 3)
    row_scale = jnp.exp(jax.random.uniform(key_rows, (TOKENS, 1), jnp.float32, -1.2, 1.2))
    col_scale = jnp.exp(jax.random.uniform(key_cols, (1, D), jnp.float32, -1.2, 1.2))
    base = jax.random.normal(key_base, (TOKENS, D), jnp.float32)
    return jnp.clip(base * row_scale * col_scale, -30.0, 30.0).astype(jnp.bfloat16)


def draw_expert_ids(key, part):
    blocks = TOKENS // T_DEV
    hot_expert = jax.random.randint(jax.random.fold_in(key, 11), (), 0, WIN)

    def one_block(block_index):
        block_key = jax.random.fold_in(jax.random.fold_in(key, 23), block_index)
        key_counts, key_order, key_noise = jax.random.split(block_key, 3)
        counts = jax.random.randint(key_counts, (WIN,), 0, CAP + 1)
        counts = jnp.where(jnp.arange(WIN) == hot_expert, CAP, counts)
        active = (jnp.arange(CAP)[None, :] < counts[:, None]).reshape(WIN * CAP).astype(jnp.int32)
        slot_rank = jnp.cumsum(active) - 1
        shuffle = jax.random.permutation(key_order, T_DEV)
        owner_token = shuffle[slot_rank % T_DEV]
        expert = jnp.arange(WIN * CAP) // CAP
        member = jnp.zeros((T_DEV, ALL_EXP), jnp.int32).at[owner_token, expert].max(active)
        priority = jax.random.randint(key_noise, (T_DEV, ALL_EXP), 1, 1024)
        outside = jnp.arange(ALL_EXP)[None, :] >= WIN
        scores = jnp.where(member > 0, 2048, jnp.where(outside, priority, 0)) * ALL_EXP + jnp.arange(ALL_EXP)[None, :]
        chosen = lax.top_k(scores, TOPK)[1]
        return chosen.astype(jnp.int32)
    routed = lax.map(one_block, jnp.arange(blocks))
    return routed.reshape(TOKENS, TOPK)


def block_scale(stream_key, shape, cuts, smallest, high):
    level, own = 1.0, jax.random.fold_in(stream_key, 6)
    for axis_at, blocks in cuts:
        steps = jnp.exp(jax.random.uniform(jax.random.fold_in(own, axis_at), (blocks,), jnp.float32, smallest / len(cuts), high / len(cuts)))
        level = level * jnp.repeat(steps, shape[axis_at] // blocks).reshape([-1 if axis == axis_at else 1 for axis in range(len(shape))])
    return level


def scatter_about(stream_key, shape, scale, most, shards=(), kind=jnp.bfloat16):
    level = block_scale(stream_key, shape, shards, -0.22, 0.18) if shards else 1.0
    array = jax.random.normal(stream_key, shape, jnp.float32) * scale * level
    return jnp.minimum(jnp.maximum(array, -most), most).astype(kind)


def setup_inputs(seed: int = 0) -> dict:
    keys = jax.random.split(jax.random.key(seed), 11)
    stream = draw_stream(jax.random.fold_in(keys[10], 71), 0)
    heads_out = scatter_about(keys[1], (TOKENS, HV), 1.0, 6.0, ((0, 32),))
    cotangent = scatter_about(keys[2], (TOKENS, D), 1.0, 6.0, ((0, 32),))
    adapter_down = scatter_about(keys[3], (RANK, HV), HV ** -0.5, 0.046875)
    adapter_raise_factor = scatter_about(keys[4], (RANK, D), 0.1, 0.59765625)
    norm_gain = jnp.clip(jax.random.uniform(keys[5], (D,), jnp.float32, 0.5, 2.0), 0.5, 2.0)
    router = scatter_about(keys[6], (ALL_EXP, D), (D // 4) ** -0.5, 0.125)
    expert_ids = draw_expert_ids(jax.random.fold_in(keys[10], 71), 0)
    w_gate_up = scatter_about(keys[8], (WIN, D, 2, HID), D ** -0.5, 0.0625, ((0, 8), (3, 4)))
    w_down = scatter_about(keys[9], (WIN, HID, D), HID ** -0.5, 0.1875, ((0, 8), (1, 4)))
    return dict(stream=stream, heads_out=heads_out, cotangent=cotangent, adapter_down=adapter_down, adapter_raise_factor=adapter_raise_factor, norm_gain=norm_gain, router=router, expert_ids=expert_ids, w_gate_up=w_gate_up, w_down=w_down)


adapter_scale_factor = 2.0
route_scale = 2.5
norm_eps = 1e-06

def gather_rows(table, where_from):
    return table[where_from]

def scatter_rows(values, where_to):
    return jnp.zeros((T_DEV, values.shape[1]), jnp.float32).at[where_to].add(values)

def expert_pass(item):
    weight_in, weight_out, rows_in, rows_grad = item
    quarter = HID // N_DP
    returned = jnp.zeros((rows_in.shape[0], D), jnp.float32)
    dot_total = jnp.zeros((rows_in.shape[0],), jnp.float32)
    for share in range(N_DP):
        joined = weight_in[:, :, share * quarter:(share + 1) * quarter].reshape(D, 2 * quarter)
        lowered = weight_out[share * quarter:(share + 1) * quarter]
        projected = jnp.dot(rows_in, joined, preferred_element_type=jnp.float32)
        gate_pre = projected[:, :quarter]
        up_pre = projected[:, quarter:]
        sigma_gate = jax.nn.sigmoid(gate_pre)
        activated = gate_pre * sigma_gate
        hidden = (activated * up_pre).astype(jnp.bfloat16)
        hidden_grad = jnp.dot(rows_grad, lowered.T, preferred_element_type=jnp.float32)
        dot_part = lax.optimization_barrier(jnp.sum(hidden.astype(jnp.float32) * hidden_grad, axis=1)).astype(jnp.bfloat16)
        pre_grad = jnp.concatenate([hidden_grad * up_pre * sigma_gate * (1.0 + gate_pre * (1.0 - sigma_gate)), hidden_grad * activated], axis=1).astype(jnp.bfloat16)
        part_rows = jnp.dot(pre_grad, joined.T, preferred_element_type=jnp.float32).astype(jnp.bfloat16)
        returned = returned + lax.optimization_barrier(part_rows).astype(jnp.float32)
        dot_total = dot_total + lax.optimization_barrier(dot_part).astype(jnp.float32)
    return (returned.astype(jnp.bfloat16), dot_total.astype(jnp.bfloat16))

def reference(stream, heads_out, cotangent, adapter_down, adapter_raise_factor, norm_gain, router, expert_ids, w_gate_up, w_down):
    hidden_code = jnp.dot(heads_out, adapter_down.T, preferred_element_type=jnp.float32).astype(jnp.bfloat16)
    combined_result = stream.astype(jnp.float32) + adapter_scale_factor * jnp.dot(hidden_code, adapter_raise_factor, preferred_element_type=jnp.float32)
    inverse = lax.rsqrt(lax.optimization_barrier(jnp.mean(combined_result * combined_result, axis=1, keepdims=True)) + norm_eps)
    normed = combined_result * inverse
    normed_in = (normed * norm_gain).astype(jnp.bfloat16)
    logits = jnp.dot(normed_in, router.T, preferred_element_type=jnp.float32)
    affinity = jax.nn.sigmoid(logits)
    chosen = jnp.take_along_axis(affinity, expert_ids, axis=1)
    affin_sum = lax.optimization_barrier(jnp.sum(chosen, axis=1, keepdims=True))
    gate_weights = route_scale * chosen / affin_sum
    blocks = TOKENS // T_DEV
    routed = expert_ids.reshape(blocks, T_DEV, TOPK)
    window_hit = routed[:, :, :, None] == jnp.arange(WIN, dtype=jnp.int32)
    member = lax.optimization_barrier(jnp.sum(window_hit.astype(jnp.int32), axis=2))
    gate_window = lax.optimization_barrier(jnp.sum(jnp.where(window_hit, gate_weights.reshape(blocks, T_DEV, TOPK)[:, :, :, None], 0.0), axis=2))
    position = jnp.cumsum(member, axis=1) - member
    slot_hit = (member[:, :, :, None] == 1) & (position[:, :, :, None] == jnp.arange(CAP, dtype=jnp.int32))
    token_slot = lax.optimization_barrier(jnp.sum(jnp.where(slot_hit, jnp.arange(T_DEV, dtype=jnp.int32)[None, :, None, None], 0), axis=1)).astype(jnp.int32)
    filled = jnp.any(slot_hit, axis=1)
    flat_slot = token_slot.reshape(blocks, WIN * CAP)
    keep = filled.reshape(blocks, WIN * CAP, 1)
    rows_in = jax.vmap(gather_rows)(normed_in.reshape(blocks, T_DEV, D), flat_slot)
    rows_grad = jax.vmap(gather_rows)(cotangent.reshape(blocks, T_DEV, D), flat_slot)
    rows_in = jnp.where(keep, rows_in, jnp.zeros_like(rows_in))
    rows_grad = jnp.where(keep, rows_grad, jnp.zeros_like(rows_grad))
    rows_in = rows_in.reshape(blocks, WIN, CAP, D).transpose(1, 0, 2, 3).reshape(WIN, blocks * CAP, D)
    rows_grad = rows_grad.reshape(blocks, WIN, CAP, D).transpose(1, 0, 2, 3).reshape(WIN, blocks * CAP, D)
    returned, slot_dots = lax.map(expert_pass, (w_gate_up, w_down, rows_in, rows_grad))
    returned = returned.reshape(WIN, blocks, CAP, D).transpose(1, 0, 2, 3).reshape(blocks, WIN * CAP, D)
    slot_dots = slot_dots.reshape(WIN, blocks, CAP).transpose(1, 0, 2)
    slot_gate = lax.optimization_barrier(jnp.sum(jnp.where(slot_hit, gate_window[:, :, :, None], 0.0), axis=1)).astype(jnp.bfloat16)
    slot_gate = lax.optimization_barrier(slot_gate)
    weighted = slot_gate.reshape(blocks, WIN * CAP, 1).astype(jnp.float32) * returned.astype(jnp.float32)
    unit_grad = jax.vmap(scatter_rows)(weighted, flat_slot).reshape(TOKENS, D)
    slot_dot = lax.optimization_barrier(jnp.sum(jnp.where(slot_hit, slot_dots.astype(jnp.float32)[:, None, :, :], 0.0), axis=3))
    gate_grad = lax.optimization_barrier(jnp.sum(jnp.where(window_hit, slot_dot[:, :, None, :], 0.0), axis=3)).reshape(TOKENS, TOPK)
    chosen_grad = route_scale * (gate_grad / affin_sum - lax.optimization_barrier(jnp.sum(gate_grad * chosen, axis=1, keepdims=True)) / (affin_sum * affin_sum))
    logit_pick = chosen_grad * chosen * (1.0 - chosen)
    choose = expert_ids[:, :, None] == jnp.arange(ALL_EXP, dtype=jnp.int32)
    logit_grad = lax.optimization_barrier(jnp.sum(jnp.where(choose, logit_pick[:, :, None], 0.0), axis=1)).astype(jnp.bfloat16)
    unit_grad = unit_grad + jnp.dot(logit_grad, router, preferred_element_type=jnp.float32)
    scaled = unit_grad * norm_gain
    residual_stream_gradient = (cotangent.astype(jnp.float32) + inverse * (scaled - normed * lax.optimization_barrier(jnp.mean(scaled * normed, axis=1, keepdims=True)))).astype(jnp.bfloat16)
    hidden_code_gradient = (adapter_scale_factor * jnp.dot(residual_stream_gradient, adapter_raise_factor.T, preferred_element_type=jnp.float32)).astype(jnp.bfloat16)
    device_group = N_DP * N_EXPERT
    raise_factor_gradient = adapter_scale_factor * jnp.dot(hidden_code.T, residual_stream_gradient, preferred_element_type=jnp.float32) / device_group
    grad_down = jnp.dot(hidden_code_gradient.T, heads_out, preferred_element_type=jnp.float32) / device_group
    return (residual_stream_gradient, grad_down, raise_factor_gradient)
```

```python
import functools

import jax
import jax.numpy as jnp
import numpy as np
from jax import lax
from jax.experimental import pallas as pl
from jax.experimental.pallas import tpu as pltpu
from jax.sharding import PartitionSpec as P

ALL_EXP = 256
CAP = 6
TILE = 16
CHUNKS = 4
LANES = 128
VMEM_ROOM = 56 * 1024 * 1024
MESH = pl.DeviceIdType.MESH
F32 = jnp.float32
BF16 = jnp.bfloat16

adapter_scale_factor = 2.0
route_scale = 2.5
norm_eps = 1e-06


def dot_nt(a, b):
    return lax.dot_general(a, b, (((1,), (1,)), ((), ())), preferred_element_type=F32)


def dot_tn(a, b):
    return lax.dot_general(a, b, (((0,), (0,)), ((), ())), preferred_element_type=F32)


def enter(n_dp, n_exp):
    d, e = lax.axis_index("dp"), lax.axis_index("expert")
    barrier = pltpu.get_barrier_semaphore()
    for j in range(1, n_exp):
        pl.semaphore_signal(barrier, inc=1, device_id=(d, e ^ j), device_id_type=MESH)
    for j in range(1, n_dp):
        pl.semaphore_signal(barrier, inc=1, device_id=(d ^ j, e), device_id_type=MESH)
    pl.semaphore_wait(barrier, n_exp + n_dp - 2)
    return d, e


def remote(src, dst, send_sem, recv_sem, device):
    copy = pltpu.make_async_remote_copy(
        src_ref=src,
        dst_ref=dst,
        send_sem=send_sem,
        recv_sem=recv_sem,
        device_id=device,
        device_id_type=MESH,
    )
    copy.start()
    return copy


def expert_kernel(
    n_dp,
    n_exp,
    p_in_ref,
    p_gr_ref,
    q_ref,
    qt_ref,
    nin_ref,
    cot_ref,
    wj_hbm,
    wd_hbm,
    out_ref,
    sent,
    got,
    rows,
    parts,
    arrived,
    back,
    back_got,
    wj,
    wd,
    w_sem,
    a_send,
    a_recv,
    g_send,
    g_recv,
    r_send,
    r_recv,
    b_send,
    b_recv,
):
    width = nin_ref.shape[1]
    slots = n_exp * CAP
    step = width // CHUNKS
    half = width // 2
    piece = half // CHUNKS
    quarter = wd.shape[0]
    load_j = pltpu.make_async_copy(wj_hbm, wj, w_sem.at[0])
    load_d = pltpu.make_async_copy(wd_hbm, wd, w_sem.at[1])
    load_j.start()
    load_d.start()
    d, e = enter(n_dp, n_exp)
    mine = pl.ds(pl.multiple_of(e * TILE, TILE), TILE)

    first = []
    for c in range(CHUNKS):
        cols = pl.ds(c * step, step)
        picked = jnp.dot(p_in_ref[...], nin_ref[:, cols], preferred_element_type=F32)
        picked += jnp.dot(p_gr_ref[...], cot_ref[:, cols], preferred_element_type=F32)
        sent[:, cols] = picked.astype(BF16)
        copies = []
        for j in range(1, n_exp):
            theirs = pl.ds(pl.multiple_of((e ^ j) * TILE, TILE), TILE)
            copies.append(
                remote(
                    sent.at[theirs, cols],
                    got.at[mine, cols],
                    a_send.at[c, j - 1],
                    a_recv.at[c, j - 1],
                    (d, e ^ j),
                )
            )
        got[mine, cols] = sent[mine, cols]
        first.append(copies)

    second = []
    for c in range(CHUNKS):
        cols = pl.ds(c * step, step)
        for copy in first[c]:
            copy.wait_recv()
        rows[d, :, cols] = jnp.dot(
            q_ref[...], got[:, cols], preferred_element_type=F32
        ).astype(BF16)
        second.append(
            [
                remote(
                    rows.at[d, :, cols],
                    rows.at[d, :, cols],
                    g_send.at[c, j - 1],
                    g_recv.at[c, j - 1],
                    (d ^ j, e),
                )
                for j in range(1, n_dp)
            ]
        )
    load_j.wait()
    load_d.wait()
    projected = jnp.zeros((n_dp * slots, 2 * quarter), F32)
    hidden_grad = jnp.zeros((n_dp * slots, quarter), F32)
    for c in range(CHUNKS):
        cols = pl.ds(c * step, step)
        for copy in second[c]:
            copy.wait_recv()
        rows_in = rows[:, :slots, cols].reshape(n_dp * slots, step)
        rows_grad = rows[:, slots:, cols].reshape(n_dp * slots, step)
        projected += jnp.dot(rows_in, wj[cols, :], preferred_element_type=F32)
        hidden_grad += dot_nt(rows_grad, wd[:, cols])
    gate_pre = projected[:, :quarter]
    up_pre = projected[:, quarter:]
    sigma_gate = jax.nn.sigmoid(gate_pre)
    activated = gate_pre * sigma_gate
    hidden = (activated * up_pre).astype(BF16)
    slot_dots = jnp.sum(hidden.astype(F32) * hidden_grad, axis=1, keepdims=True)
    pre_grad = jnp.concatenate(
        [
            hidden_grad * up_pre * sigma_gate * (1.0 + gate_pre * (1.0 - sigma_gate)),
            hidden_grad * activated,
        ],
        axis=1,
    ).astype(BF16)

    spans = [(width, LANES, half, False)]
    spans += [(c * 2 * piece, 2 * piece, c * piece, True) for c in range(CHUNKS)]
    third = []
    for c, (at, size, _, real) in enumerate(spans):
        if real:
            low = (c - 1) * piece
            part = jnp.concatenate(
                [
                    dot_nt(pre_grad, wj[pl.ds(low, piece), :]),
                    dot_nt(pre_grad, wj[pl.ds(half + low, piece), :]),
                ],
                axis=1,
            )
        else:
            part = jnp.broadcast_to(slot_dots, (n_dp * slots, LANES))
        parts[:, :, pl.ds(at, size)] = part.astype(BF16).reshape(n_dp, slots, size)
        third.append(
            [
                remote(
                    parts.at[d ^ j, :, pl.ds(at, size)],
                    arrived.at[j - 1, :, pl.ds(at, size)],
                    r_send.at[c, j - 1],
                    r_recv.at[c, j - 1],
                    (d ^ j, e),
                )
                for j in range(1, n_dp)
            ]
        )
    fourth = []
    for c, (at, size, low, real) in enumerate(spans):
        for copy in third[c]:
            copy.wait_recv()
        total = parts[d, :, pl.ds(at, size)].astype(F32)
        for j in range(1, n_dp):
            total += arrived[j - 1, :, pl.ds(at, size)].astype(F32)
        total = total.astype(BF16)
        if real:
            spread = jnp.dot(qt_ref[:, :slots], total[:, :piece], preferred_element_type=F32)
            spread += jnp.dot(qt_ref[:, slots:], total[:, piece:], preferred_element_type=F32)
        else:
            spread = jnp.dot(qt_ref[:, :slots], total, preferred_element_type=F32)
        cols = pl.ds(low, spread.shape[1])
        back[:, cols] = spread.astype(BF16)
        copies = []
        for j in range(1, n_exp):
            theirs = pl.ds(pl.multiple_of((e ^ j) * TILE, TILE), TILE)
            copies.append(
                remote(
                    back.at[theirs, cols],
                    back_got.at[mine, cols],
                    b_send.at[c, j - 1],
                    b_recv.at[c, j - 1],
                    (d, e ^ j),
                )
            )
        back_got[mine, cols] = back[mine, cols]
        fourth.append(copies)
    for c, (_, size, low, real) in enumerate(spans):
        for copy in fourth[c]:
            copy.wait_recv()
        cols = pl.ds(low, piece if real else size)
        out_ref[:, cols] = back_got[:, cols]
    for stage in (first, second, third, fourth):
        for copies in stage:
            for copy in copies:
                copy.wait_send()


def expert_buffers(n_dp, n_exp, width, quarter):
    slots, padded = n_exp * CAP, n_exp * TILE
    return [
        ((padded, width), BF16),
        ((padded, width), BF16),
        ((n_dp, 2 * slots, width), BF16),
        ((n_dp, slots, width + LANES), BF16),
        ((n_dp - 1, slots, width + LANES), BF16),
        ((padded, width // 2 + LANES), BF16),
        ((padded, width // 2 + LANES), BF16),
        ((width, 2 * quarter), BF16),
        ((quarter, width), BF16),
    ]


def expert_exchange(p_in, p_gr, normed_in, cotangent, joined, lowered, n_dp, n_exp):
    width = normed_in.shape[1]
    quarter = lowered.shape[0]
    slots, padded = n_exp * CAP, n_exp * TILE
    squeeze = np.zeros((2 * slots, padded), np.float32)
    for kind in range(2):
        for e in range(n_exp):
            for s in range(CAP):
                squeeze[kind * slots + e * CAP + s, e * TILE + kind * CAP + s] = 1.0
    vmem = pl.BlockSpec(memory_space=pltpu.VMEM)
    dma = pltpu.SemaphoreType.DMA
    return pl.pallas_call(
        functools.partial(expert_kernel, n_dp, n_exp),
        out_shape=jax.ShapeDtypeStruct((padded, width // 2 + LANES), BF16),
        in_specs=[vmem] * 6 + [pl.BlockSpec(memory_space=pl.ANY)] * 2,
        out_specs=vmem,
        scratch_shapes=[
            pltpu.VMEM(shape, kind)
            for shape, kind in expert_buffers(n_dp, n_exp, width, quarter)
        ]
        + [
            dma((2,)),
            dma((CHUNKS, n_exp - 1)),
            dma((CHUNKS, n_exp - 1)),
            dma((CHUNKS, n_dp - 1)),
            dma((CHUNKS, n_dp - 1)),
            dma((CHUNKS + 1, n_dp - 1)),
            dma((CHUNKS + 1, n_dp - 1)),
            dma((CHUNKS + 1, n_exp - 1)),
            dma((CHUNKS + 1, n_exp - 1)),
        ],
        compiler_params=pltpu.CompilerParams(
            collective_id=0, has_side_effects=True, vmem_limit_bytes=VMEM_ROOM
        ),
    )(
        p_in,
        p_gr,
        jnp.asarray(squeeze, BF16),
        jnp.asarray(squeeze.T, BF16),
        normed_in,
        cotangent,
        joined,
        lowered,
    )


def reduce_kernel(
    n_dp,
    n_exp,
    x_ref,
    o_ref,
    y,
    z,
    v,
    b,
    y_send,
    y_recv,
    v_send,
    v_recv,
    c_send,
    c_recv,
    d_send,
    d_recv,
):
    wide = x_ref.shape[1] // n_dp
    share = wide // n_exp
    d, e = enter(n_dp, n_exp)

    def block(i):
        return pl.ds(pl.multiple_of(i * wide, LANES), wide)

    def small(i):
        return pl.ds(pl.multiple_of(i * share, LANES), share)

    first = [
        remote(
            x_ref.at[:, block(d ^ j)],
            y.at[j - 1],
            y_send.at[j - 1],
            y_recv.at[j - 1],
            (d ^ j, e),
        )
        for j in range(1, n_dp)
    ]
    for copy in first:
        copy.wait_recv()
    total = x_ref[:, block(d)].astype(F32)
    for j in range(1, n_dp):
        total += y[j - 1].astype(F32)
    z[...] = total.astype(BF16)
    second = [
        remote(
            z.at[:, small(e ^ j)],
            v.at[j - 1],
            v_send.at[j - 1],
            v_recv.at[j - 1],
            (d, e ^ j),
        )
        for j in range(1, n_exp)
    ]
    for copy in second:
        copy.wait_recv()
    total = z[:, small(e)].astype(F32)
    for j in range(1, n_exp):
        total += v[j - 1].astype(F32)
    own = small(d * n_exp + e)
    b[:, own] = total.astype(BF16)
    third = [
        remote(b.at[:, own], b.at[:, own], c_send.at[j - 1], c_recv.at[j - 1], (d, e ^ j))
        for j in range(1, n_exp)
    ]
    for copy in third:
        copy.wait_recv()
    fourth = [
        remote(
            b.at[:, block(d)], b.at[:, block(d)], d_send.at[j - 1], d_recv.at[j - 1], (d ^ j, e)
        )
        for j in range(1, n_dp)
    ]
    for copy in fourth:
        copy.wait_recv()
    o_ref[...] = b[...].astype(F32) * (1.0 / (n_dp * n_exp))
    for copies in (first, second, third, fourth):
        for copy in copies:
            copy.wait_send()


def mean_over_devices(terms, n_dp, n_exp):
    rank = terms[0].shape[0]
    total = sum(t.shape[1] for t in terms)
    devices = n_dp * n_exp
    share = -(-total // (devices * LANES)) * LANES
    width = share * devices
    x = jnp.concatenate(
        [t.astype(BF16) for t in terms] + [jnp.zeros((rank, width - total), BF16)], axis=1
    )
    vmem = pl.BlockSpec(memory_space=pltpu.VMEM)
    dma = pltpu.SemaphoreType.DMA
    out = pl.pallas_call(
        functools.partial(reduce_kernel, n_dp, n_exp),
        out_shape=jax.ShapeDtypeStruct((rank, width), F32),
        in_specs=[vmem],
        out_specs=vmem,
        scratch_shapes=[
            pltpu.VMEM((n_dp - 1, rank, width // n_dp), BF16),
            pltpu.VMEM((rank, width // n_dp), BF16),
            pltpu.VMEM((n_exp - 1, rank, share), BF16),
            pltpu.VMEM((rank, width), BF16),
            dma((n_dp - 1,)),
            dma((n_dp - 1,)),
            dma((n_exp - 1,)),
            dma((n_exp - 1,)),
            dma((n_exp - 1,)),
            dma((n_exp - 1,)),
            dma((n_dp - 1,)),
            dma((n_dp - 1,)),
        ],
        compiler_params=pltpu.CompilerParams(
            collective_id=1, has_side_effects=True, vmem_limit_bytes=VMEM_ROOM
        ),
    )(x)
    at, outs = 0, []
    for t in terms:
        outs.append(out[:, at : at + t.shape[1]])
        at += t.shape[1]
    return outs


def expert_rows(rows_in, rows_grad, w_gate_up, w_down):
    quarter = w_down.shape[1]
    width = w_down.shape[2]
    flat_in = rows_in.reshape(-1, width)
    flat_grad = rows_grad.reshape(-1, width)
    joined = w_gate_up.reshape(width, 2 * quarter)
    lowered = w_down.reshape(quarter, width)
    projected = jnp.dot(flat_in, joined, preferred_element_type=jnp.float32)
    gate_pre = projected[:, :quarter]
    up_pre = projected[:, quarter:]
    sigma_gate = jax.nn.sigmoid(gate_pre)
    activated = gate_pre * sigma_gate
    hidden = (activated * up_pre).astype(jnp.bfloat16)
    hidden_grad = jnp.einsum("md,hd->mh", flat_grad, lowered, preferred_element_type=jnp.float32)
    slot_dots = jnp.sum(hidden.astype(jnp.float32) * hidden_grad, axis=1)
    pre_grad = jnp.concatenate(
        [
            hidden_grad * up_pre * sigma_gate * (1.0 + gate_pre * (1.0 - sigma_gate)),
            hidden_grad * activated,
        ],
        axis=1,
    ).astype(jnp.bfloat16)
    partial_rows = jnp.einsum("mk,dk->md", pre_grad, joined, preferred_element_type=jnp.float32)
    return (partial_rows, slot_dots)


def exchange_by_collectives(pick, normed_in, cotangent, w_gate_up, w_down):
    width = normed_in.shape[1]
    experts_here, replicas = lax.axis_size("expert"), lax.axis_size("dp")
    gathered = []
    for rows in (normed_in, cotangent):
        send = jnp.dot(pick, rows, preferred_element_type=F32).astype(BF16)
        got = lax.all_to_all(
            send.reshape(experts_here, CAP, width), "expert", 0, 0, tiled=True
        )
        gathered.append(lax.all_gather(got, "dp", axis=0, tiled=True))
    partial_rows, slot_dots = expert_rows(*gathered, w_gate_up, w_down)
    sums = []
    for part in (partial_rows, slot_dots[:, None]):
        part = part.astype(BF16).reshape(replicas * experts_here, CAP, -1)
        part = lax.psum_scatter(part, "dp", scatter_dimension=0, tiled=True)
        part = lax.all_to_all(part.astype(BF16), "expert", 0, 0, tiled=True)
        sums.append(part)
    return sums[0].reshape(experts_here * CAP, width), sums[1][:, :, 0].astype(F32)


def local(
    stream,
    heads_out,
    cotangent,
    adapter_down,
    adapter_raise_factor,
    norm_gain,
    router,
    expert_ids,
    w_gate_up,
    w_down,
):
    tokens_here = stream.shape[0]
    width = stream.shape[1]
    experts_here = lax.axis_size("expert")
    replicas = lax.axis_size("dp")
    hidden_code = jnp.einsum(
        "th,rh->tr", heads_out, adapter_down, preferred_element_type=jnp.float32
    ).astype(jnp.bfloat16)
    combined_result = stream.astype(jnp.float32) + adapter_scale_factor * jnp.dot(
        hidden_code, adapter_raise_factor, preferred_element_type=jnp.float32
    )
    inverse = lax.rsqrt(
        jnp.mean(combined_result * combined_result, axis=1, keepdims=True) + norm_eps
    )
    normed = combined_result * inverse
    normed_in = (normed * norm_gain).astype(jnp.bfloat16)
    logits = jnp.einsum("td,ed->te", normed_in, router, preferred_element_type=jnp.float32)
    affinity = jax.nn.sigmoid(logits)
    choose = expert_ids[:, :, None] == jnp.arange(ALL_EXP, dtype=jnp.int32)[None, None, :]
    chosen = jnp.sum(jnp.where(choose, affinity[:, None, :], 0.0), axis=2)
    affin_sum = jnp.sum(chosen, axis=1, keepdims=True)
    gate_weights = route_scale * chosen / affin_sum
    window = jnp.arange(experts_here, dtype=jnp.int32)
    window_hit = expert_ids[:, :, None] == window[None, None, :]
    hit_any = jnp.sum(window_hit.astype(jnp.int32), axis=1).T
    gate_window = jnp.sum(jnp.where(window_hit, gate_weights[:, :, None], 0.0), axis=1).T
    token = jnp.arange(tokens_here, dtype=jnp.int32)
    earlier = (token[:, None] < token[None, :]).astype(jnp.bfloat16)
    before = jnp.dot(
        hit_any.astype(jnp.bfloat16), earlier, preferred_element_type=jnp.float32
    ).astype(jnp.int32)
    position = jnp.where(hit_any == 1, before, -ALL_EXP)
    slot = jnp.arange(TILE, dtype=jnp.int32)[None, :, None]
    pick_low = position[:, None, :] == slot
    pick_high = position[:, None, :] == slot - CAP
    padded = experts_here * TILE
    joined = w_gate_up.reshape(width, -1)
    lowered = w_down.reshape(-1, width)
    buffers = expert_buffers(replicas, experts_here, width, lowered.shape[0])
    if sum(int(np.prod(shape)) * 2 for shape, _ in buffers) < 0.75 * VMEM_ROOM:
        answer = expert_exchange(
            pick_low.reshape(padded, tokens_here).astype(jnp.bfloat16),
            pick_high.reshape(padded, tokens_here).astype(jnp.bfloat16),
            normed_in,
            cotangent,
            joined,
            lowered,
            replicas,
            experts_here,
        )
        returned = answer[:, : width // 2]
        dot_sum = answer[:, width // 2].astype(jnp.float32).reshape(experts_here, TILE, 1)
        weights = [
            jnp.where(pick, gate_window[:, None, :], 0.0)
            .reshape(padded, tokens_here)
            .astype(jnp.bfloat16)
            for pick in (pick_low, pick_high)
        ]
        unit_grad = jnp.concatenate([dot_tn(w, returned) for w in weights], axis=1)
        slot_dot = jnp.sum(jnp.where(pick_low, dot_sum, 0.0), axis=1).T
    else:
        pick = pick_low[:, :CAP].reshape(-1, tokens_here)
        returned, dot_sum = exchange_by_collectives(
            pick.astype(jnp.bfloat16), normed_in, cotangent, w_gate_up, w_down
        )
        weights = jnp.where(pick_low[:, :CAP], gate_window[:, None, :], 0.0)
        unit_grad = dot_tn(weights.reshape(-1, tokens_here).astype(jnp.bfloat16), returned)
        slot_dot = jnp.sum(jnp.where(pick_low[:, :CAP], dot_sum[:, :, None], 0.0), axis=1).T
    gate_grad = jnp.sum(jnp.where(window_hit, slot_dot[:, None, :], 0.0), axis=2)
    chosen_grad = route_scale * (
        gate_grad / affin_sum
        - jnp.sum(gate_grad * chosen, axis=1, keepdims=True) / (affin_sum * affin_sum)
    )
    logit_pick = chosen_grad * chosen * (1.0 - chosen)
    logit_grad = jnp.sum(jnp.where(choose, logit_pick[:, :, None], 0.0), axis=1).astype(
        jnp.bfloat16
    )
    unit_grad = unit_grad + jnp.dot(logit_grad, router, preferred_element_type=jnp.float32)
    scaled = unit_grad * norm_gain
    residual_stream_gradient = (
        cotangent.astype(jnp.float32)
        + inverse * (scaled - normed * jnp.mean(scaled * normed, axis=1, keepdims=True))
    ).astype(jnp.bfloat16)
    hidden_code_gradient = (
        adapter_scale_factor
        * jnp.einsum(
            "td,rd->tr",
            residual_stream_gradient,
            adapter_raise_factor,
            preferred_element_type=jnp.float32,
        )
    ).astype(jnp.bfloat16)
    partial_raise_sum = adapter_scale_factor * jnp.einsum(
        "tr,td->rd", hidden_code, residual_stream_gradient, preferred_element_type=jnp.float32
    )
    part_down = jnp.einsum(
        "tr,th->rh", hidden_code_gradient, heads_out, preferred_element_type=jnp.float32
    )
    mean_down, mean_up = mean_over_devices(
        (part_down, partial_raise_sum), replicas, experts_here
    )
    return (residual_stream_gradient, mean_down, mean_up)


def solution(mesh):
    return jax.shard_map(
        local,
        mesh=mesh,
        in_specs=(
            P(("dp", "expert"), None),
            P(("dp", "expert"), None),
            P(("dp", "expert"), None),
            P(),
            P(),
            P(),
            P(),
            P(("dp", "expert"), None),
            P("expert", None, None, "dp"),
            P("expert", "dp", None),
        ),
        out_specs=(P(("dp", "expert"), None), P(), P()),
        check_vma=False,
    )
```

```python
import functools

import jax
import jax.numpy as jnp
import numpy as np
from jax import lax
from jax.experimental import pallas as pl
from jax.experimental.pallas import tpu as pltpu
from jax.sharding import PartitionSpec as P

ALL_EXP = 256
CAP = 6
TILE = 16
CHUNKS = 7
LANES = 128
VMEM_ROOM = 56 * 1024 * 1024
MESH = pl.DeviceIdType.MESH
F32 = jnp.float32
BF16 = jnp.bfloat16

adapter_scale_factor = 2.0
route_scale = 2.5
norm_eps = 1e-06


def dot_nt(a, b):
    return lax.dot_general(a, b, (((1,), (1,)), ((), ())), preferred_element_type=F32)


def dot_tn(a, b):
    return lax.dot_general(a, b, (((0,), (0,)), ((), ())), preferred_element_type=F32)


def enter(n_dp, n_exp):
    d, e = lax.axis_index("dp"), lax.axis_index("expert")
    barrier = pltpu.get_barrier_semaphore()
    for j in range(1, n_exp):
        pl.semaphore_signal(barrier, inc=1, device_id=(d, e ^ j), device_id_type=MESH)
    for j in range(1, n_dp):
        pl.semaphore_signal(barrier, inc=1, device_id=(d ^ j, e), device_id_type=MESH)
    pl.semaphore_wait(barrier, n_exp + n_dp - 2)
    return d, e


def remote(src, dst, send_sem, recv_sem, device):
    copy = pltpu.make_async_remote_copy(
        src_ref=src,
        dst_ref=dst,
        send_sem=send_sem,
        recv_sem=recv_sem,
        device_id=device,
        device_id_type=MESH,
    )
    copy.start()
    return copy


def expert_kernel(
    n_dp,
    n_exp,
    p_in_ref,
    p_gr_ref,
    q_ref,
    qt_ref,
    nin_ref,
    cot_ref,
    wj_hbm,
    wd_hbm,
    out_ref,
    sent,
    got,
    rows,
    parts,
    arrived,
    back,
    back_got,
    wj,
    wd,
    w_sem,
    a_send,
    a_recv,
    g_send,
    g_recv,
    r_send,
    r_recv,
    b_send,
    b_recv,
):
    width = nin_ref.shape[1]
    slots = n_exp * CAP
    step = width // CHUNKS
    half = width // 2
    piece = half // CHUNKS
    quarter = wd.shape[0]
    load_j = pltpu.make_async_copy(wj_hbm, wj, w_sem.at[0])
    load_d = pltpu.make_async_copy(wd_hbm, wd, w_sem.at[1])
    load_j.start()
    load_d.start()
    d, e = enter(n_dp, n_exp)
    mine = pl.ds(pl.multiple_of(e * TILE, TILE), TILE)

    first = []
    for c in range(CHUNKS):
        cols = pl.ds(c * step, step)
        picked = jnp.dot(p_in_ref[...], nin_ref[:, cols], preferred_element_type=F32)
        picked += jnp.dot(p_gr_ref[...], cot_ref[:, cols], preferred_element_type=F32)
        sent[:, cols] = picked.astype(BF16)
        copies = []
        for j in range(1, n_exp):
            theirs = pl.ds(pl.multiple_of((e ^ j) * TILE, TILE), TILE)
            copies.append(
                remote(
                    sent.at[theirs, cols],
                    got.at[mine, cols],
                    a_send.at[c, j - 1],
                    a_recv.at[c, j - 1],
                    (d, e ^ j),
                )
            )
        got[mine, cols] = sent[mine, cols]
        first.append(copies)

    second, relayed = [], []
    for c in range(CHUNKS + 1):
        if c < CHUNKS:
            cols = pl.ds(c * step, step)
            for copy in first[c]:
                copy.wait_recv()
            rows[0, :, cols] = jnp.dot(
                q_ref[...], got[:, cols], preferred_element_type=F32
            ).astype(BF16)
            second.append(
                [
                    remote(
                        rows.at[0, :, cols],
                        rows.at[j, :, cols],
                        g_send.at[c, j - 1],
                        g_recv.at[c, j - 1],
                        (d ^ j, e),
                    )
                    for j in (1, 2)
                ]
            )
        if c > 0:
            cols = pl.ds((c - 1) * step, step)
            copies = []
            for j in (1, 2):
                second[c - 1][j - 1].wait_recv()
                some = pl.ds((j - 1) * slots, slots)
                copies.append(
                    remote(
                        rows.at[j, some, cols],
                        rows.at[3, some, cols],
                        g_send.at[c - 1, j + 1],
                        g_recv.at[c - 1, j + 1],
                        (d ^ (3 - j), e),
                    )
                )
            relayed.append(copies)
    load_j.wait()
    load_d.wait()
    projected = jnp.zeros((n_dp * slots, 2 * quarter), F32)
    hidden_grad = jnp.zeros((n_dp * slots, quarter), F32)
    for c in range(CHUNKS):
        cols = pl.ds(c * step, step)
        for copy in relayed[c]:
            copy.wait_recv()
        rows_in = rows[:, :slots, cols].reshape(n_dp * slots, step)
        rows_grad = rows[:, slots:, cols].reshape(n_dp * slots, step)
        projected += jnp.dot(rows_in, wj[cols, :], preferred_element_type=F32)
        hidden_grad += dot_nt(rows_grad, wd[:, cols])
    gate_pre = projected[:, :quarter]
    up_pre = projected[:, quarter:]
    sigma_gate = jax.nn.sigmoid(gate_pre)
    activated = gate_pre * sigma_gate
    hidden = (activated * up_pre).astype(BF16)
    slot_dots = jnp.sum(hidden.astype(F32) * hidden_grad, axis=1, keepdims=True)
    pre_grad = jnp.concatenate(
        [
            hidden_grad * up_pre * sigma_gate * (1.0 + gate_pre * (1.0 - sigma_gate)),
            hidden_grad * activated,
        ],
        axis=1,
    ).astype(BF16)

    spans = [(width, LANES, half, False)]
    spans += [(c * 2 * piece, piece, c * piece, True) for c in range(CHUNKS)]
    count = len(spans)
    third, passed, fourth = [], [], []
    for turn in range(count + 2):
        if turn < count:
            c = turn
            at, size, low, real = spans[c]
            copies = []
            for j in (1, 2) if real else (1,):
                cols = pl.ds(at + (j - 1) * size, size)
                if real:
                    part = dot_nt(pre_grad, wj[pl.ds((j - 1) * half + low, size), :])
                else:
                    part = jnp.broadcast_to(slot_dots, (n_dp * slots, LANES))
                parts[:, :, cols] = part.astype(BF16).reshape(n_dp, slots, size)
                copies.append(
                    [
                        remote(
                            parts.at[block, :, cols],
                            arrived.at[place, :, cols],
                            r_send.at[c, j - 1, place],
                            r_recv.at[c, j - 1, place],
                            (d ^ j, e),
                        )
                        for place, block in ((1, 3), (0, j))
                    ]
                )
            third.append(copies)
        if 0 < turn <= count:
            c = turn - 1
            at, size, low, real = spans[c]
            copies = []
            for j in (1, 2) if real else (1,):
                cols = pl.ds(at + (j - 1) * size, size)
                other = 3 - j
                for copy in third[c][j - 1]:
                    copy.wait_recv()
                both = parts[other, :, cols].astype(F32) + arrived[1, :, cols].astype(F32)
                parts[other, :, cols] = both.astype(BF16)
                copies.append(
                    remote(
                        parts.at[other, :, cols],
                        arrived.at[2, :, cols],
                        r_send.at[c, j - 1, 2],
                        r_recv.at[c, j - 1, 2],
                        (d ^ other, e),
                    )
                )
            passed.append(copies)
        if turn >= 2:
            c = turn - 2
            at, size, low, real = spans[c]
            spread = jnp.zeros((n_exp * TILE, size), F32)
            for j in (1, 2) if real else (1,):
                cols = pl.ds(at + (j - 1) * size, size)
                passed[c][j - 1].wait_recv()
                total = parts[0, :, cols].astype(F32) + arrived[0, :, cols].astype(F32)
                total = (total + arrived[2, :, cols].astype(F32)).astype(BF16)
                spread += jnp.dot(
                    qt_ref[j - 1], total, preferred_element_type=F32
                )
            cols = pl.ds(low, size)
            back[:, cols] = spread.astype(BF16)
            copies = []
            for j in range(1, n_exp):
                theirs = pl.ds(pl.multiple_of((e ^ j) * TILE, TILE), TILE)
                copies.append(
                    remote(
                        back.at[theirs, cols],
                        back_got.at[mine, cols],
                        b_send.at[c, j - 1],
                        b_recv.at[c, j - 1],
                        (d, e ^ j),
                    )
                )
            back_got[mine, cols] = back[mine, cols]
            fourth.append(copies)
    for c, (_, size, low, real) in enumerate(spans):
        for copy in fourth[c]:
            copy.wait_recv()
        cols = pl.ds(low, size)
        out_ref[:, cols] = back_got[:, cols]
    third = [sum(copies, []) for copies in third]
    for stage in (first, second, relayed, third, passed, fourth):
        for copies in stage:
            for copy in copies:
                copy.wait_send()


def expert_buffers(n_dp, n_exp, width, quarter):
    slots, padded = n_exp * CAP, n_exp * TILE
    return [
        ((padded, width), BF16),
        ((padded, width), BF16),
        ((n_dp, 2 * slots, width), BF16),
        ((n_dp, slots, width + LANES), BF16),
        ((n_dp - 1, slots, width + LANES), BF16),
        ((padded, width // 2 + LANES), BF16),
        ((padded, width // 2 + LANES), BF16),
        ((width, 2 * quarter), BF16),
        ((quarter, width), BF16),
    ]


def expert_exchange(p_in, p_gr, normed_in, cotangent, joined, lowered, n_dp, n_exp):
    width = normed_in.shape[1]
    quarter = lowered.shape[0]
    slots, padded = n_exp * CAP, n_exp * TILE
    squeeze = np.zeros((2 * slots, padded), np.float32)
    for kind in range(2):
        for e in range(n_exp):
            for s in range(CAP):
                squeeze[kind * slots + e * CAP + s, e * TILE + kind * CAP + s] = 1.0
    vmem = pl.BlockSpec(memory_space=pltpu.VMEM)
    dma = pltpu.SemaphoreType.DMA
    return pl.pallas_call(
        functools.partial(expert_kernel, n_dp, n_exp),
        out_shape=jax.ShapeDtypeStruct((padded, width // 2 + LANES), BF16),
        in_specs=[vmem] * 6 + [pl.BlockSpec(memory_space=pl.ANY)] * 2,
        out_specs=vmem,
        scratch_shapes=[
            pltpu.VMEM(shape, kind)
            for shape, kind in expert_buffers(n_dp, n_exp, width, quarter)
        ]
        + [
            dma((2,)),
            dma((CHUNKS, n_exp - 1)),
            dma((CHUNKS, n_exp - 1)),
            dma((CHUNKS, 4)),
            dma((CHUNKS, 4)),
            dma((CHUNKS + 1, 2, 3)),
            dma((CHUNKS + 1, 2, 3)),
            dma((CHUNKS + 1, n_exp - 1)),
            dma((CHUNKS + 1, n_exp - 1)),
        ],
        compiler_params=pltpu.CompilerParams(
            collective_id=0, has_side_effects=True, vmem_limit_bytes=VMEM_ROOM
        ),
    )(
        p_in,
        p_gr,
        jnp.asarray(squeeze, BF16),
        jnp.asarray(squeeze.reshape(2, slots, padded).transpose(0, 2, 1), BF16),
        normed_in,
        cotangent,
        joined,
        lowered,
    )


def reduce_kernel(n_dp, n_exp, x_ref, o_ref, *scratch):
    d, e = enter(n_dp, n_exp)
    pairs = n_exp // 2
    groups = [
        (2, e & 1, lambda j: (d, e ^ j)),
        (n_dp, d, lambda j: (d ^ j, e)),
        (pairs, e >> 1, lambda j: (d, e ^ (2 * j))),
    ]
    started = []
    held, size, base, bases = x_ref, x_ref.shape[1], 0, []
    for k, (n, index, partner) in enumerate(groups):
        got, total_ref, send, recv = scratch[4 * k : 4 * k + 4]
        size //= n

        def part(i, size=size):
            return pl.ds(pl.multiple_of(i * size, LANES), size)

        copies = [
            remote(
                held.at[:, part(index ^ j)],
                got.at[j - 1],
                send.at[0, j - 1],
                recv.at[0, j - 1],
                partner(j),
            )
            for j in range(1, n)
        ]
        for copy in copies:
            copy.wait_recv()
        started += copies
        total = held[:, part(index)].astype(F32)
        for j in range(1, n):
            total += got[j - 1].astype(F32)
        total_ref[...] = total.astype(BF16)
        held = total_ref
        base = base + index * size
        bases.append((base, size))
    base, size = bases[-1]
    o_ref[:, pl.ds(pl.multiple_of(base, LANES), size)] = held[...]
    for k in reversed(range(3)):
        n, _, partner = groups[k]
        _, _, send, recv = scratch[4 * k : 4 * k + 4]
        base, size = bases[k]
        own = pl.ds(pl.multiple_of(base, LANES), size)
        copies = [
            remote(
                o_ref.at[:, own], o_ref.at[:, own], send.at[1, j - 1], recv.at[1, j - 1], partner(j)
            )
            for j in range(1, n)
        ]
        for copy in copies:
            copy.wait_recv()
        started += copies
    for copy in started:
        copy.wait_send()


def mean_over_devices(terms, n_dp, n_exp):
    rank = terms[0].shape[0]
    total = sum(t.shape[1] for t in terms)
    devices = n_dp * n_exp
    share = -(-total // (devices * LANES)) * LANES
    width = share * devices
    x = jnp.concatenate(
        [t.astype(BF16) for t in terms] + [jnp.zeros((rank, width - total), BF16)], axis=1
    )
    vmem = pl.BlockSpec(memory_space=pltpu.VMEM)
    dma = pltpu.SemaphoreType.DMA
    scratch, size = [], width
    for n in (2, n_dp, n_exp // 2):
        size //= n
        scratch += [pltpu.VMEM((n - 1, rank, size), BF16), pltpu.VMEM((rank, size), BF16)]
        scratch += [dma((2, n - 1)), dma((2, n - 1))]
    out = pl.pallas_call(
        functools.partial(reduce_kernel, n_dp, n_exp),
        out_shape=jax.ShapeDtypeStruct((rank, width), BF16),
        in_specs=[vmem],
        out_specs=vmem,
        scratch_shapes=scratch,
        compiler_params=pltpu.CompilerParams(
            collective_id=1, has_side_effects=True, vmem_limit_bytes=VMEM_ROOM
        ),
    )(x)
    at, outs = 0, []
    for t in terms:
        outs.append(out[:, at : at + t.shape[1]].astype(F32) / devices)
        at += t.shape[1]
    return outs


def expert_rows(rows_in, rows_grad, w_gate_up, w_down):
    quarter = w_down.shape[1]
    width = w_down.shape[2]
    flat_in = rows_in.reshape(-1, width)
    flat_grad = rows_grad.reshape(-1, width)
    joined = w_gate_up.reshape(width, 2 * quarter)
    lowered = w_down.reshape(quarter, width)
    projected = jnp.dot(flat_in, joined, preferred_element_type=jnp.float32)
    gate_pre = projected[:, :quarter]
    up_pre = projected[:, quarter:]
    sigma_gate = jax.nn.sigmoid(gate_pre)
    activated = gate_pre * sigma_gate
    hidden = (activated * up_pre).astype(jnp.bfloat16)
    hidden_grad = jnp.einsum("md,hd->mh", flat_grad, lowered, preferred_element_type=jnp.float32)
    slot_dots = jnp.sum(hidden.astype(jnp.float32) * hidden_grad, axis=1)
    pre_grad = jnp.concatenate(
        [
            hidden_grad * up_pre * sigma_gate * (1.0 + gate_pre * (1.0 - sigma_gate)),
            hidden_grad * activated,
        ],
        axis=1,
    ).astype(jnp.bfloat16)
    partial_rows = jnp.einsum("mk,dk->md", pre_grad, joined, preferred_element_type=jnp.float32)
    return (partial_rows, slot_dots)


def exchange_by_collectives(pick, normed_in, cotangent, w_gate_up, w_down):
    width = normed_in.shape[1]
    experts_here, replicas = lax.axis_size("expert"), lax.axis_size("dp")
    gathered = []
    for rows in (normed_in, cotangent):
        send = jnp.dot(pick, rows, preferred_element_type=F32).astype(BF16)
        got = lax.all_to_all(
            send.reshape(experts_here, CAP, width), "expert", 0, 0, tiled=True
        )
        gathered.append(lax.all_gather(got, "dp", axis=0, tiled=True))
    partial_rows, slot_dots = expert_rows(*gathered, w_gate_up, w_down)
    sums = []
    for part in (partial_rows, slot_dots[:, None]):
        part = part.astype(BF16).reshape(replicas * experts_here, CAP, -1)
        part = lax.psum_scatter(part, "dp", scatter_dimension=0, tiled=True)
        part = lax.all_to_all(part.astype(BF16), "expert", 0, 0, tiled=True)
        sums.append(part)
    return sums[0].reshape(experts_here * CAP, width), sums[1][:, :, 0].astype(F32)


def local(
    stream,
    heads_out,
    cotangent,
    adapter_down,
    adapter_raise_factor,
    norm_gain,
    router,
    expert_ids,
    w_gate_up,
    w_down,
):
    tokens_here = stream.shape[0]
    width = stream.shape[1]
    experts_here = lax.axis_size("expert")
    replicas = lax.axis_size("dp")
    hidden_code = jnp.einsum(
        "th,rh->tr", heads_out, adapter_down, preferred_element_type=jnp.float32
    ).astype(jnp.bfloat16)
    combined_result = stream.astype(jnp.float32) + adapter_scale_factor * jnp.dot(
        hidden_code, adapter_raise_factor, preferred_element_type=jnp.float32
    )
    inverse = lax.rsqrt(
        jnp.mean(combined_result * combined_result, axis=1, keepdims=True) + norm_eps
    )
    normed = combined_result * inverse
    normed_in = (normed * norm_gain).astype(jnp.bfloat16)
    logits = jnp.einsum("td,ed->te", normed_in, router, preferred_element_type=jnp.float32)
    affinity = jax.nn.sigmoid(logits)
    choose = expert_ids[:, :, None] == jnp.arange(ALL_EXP, dtype=jnp.int32)[None, None, :]
    chosen = jnp.sum(jnp.where(choose, affinity[:, None, :], 0.0), axis=2)
    affin_sum = jnp.sum(chosen, axis=1, keepdims=True)
    gate_weights = route_scale * chosen / affin_sum
    window = jnp.arange(experts_here, dtype=jnp.int32)
    window_hit = expert_ids[:, :, None] == window[None, None, :]
    hit_any = jnp.sum(window_hit.astype(jnp.int32), axis=1).T
    gate_window = jnp.sum(jnp.where(window_hit, gate_weights[:, :, None], 0.0), axis=1).T
    token = jnp.arange(tokens_here, dtype=jnp.int32)
    earlier = (token[:, None] < token[None, :]).astype(jnp.bfloat16)
    before = jnp.dot(
        hit_any.astype(jnp.bfloat16), earlier, preferred_element_type=jnp.float32
    ).astype(jnp.int32)
    position = jnp.where(hit_any == 1, before, -ALL_EXP)
    slot = jnp.arange(TILE, dtype=jnp.int32)[None, :, None]
    pick_low = position[:, None, :] == slot
    pick_high = position[:, None, :] == slot - CAP
    padded = experts_here * TILE
    joined = w_gate_up.reshape(width, -1)
    lowered = w_down.reshape(-1, width)
    buffers = expert_buffers(replicas, experts_here, width, lowered.shape[0])
    fits = replicas == 4 and sum(int(np.prod(shape)) * 2 for shape, _ in buffers) < 0.75 * VMEM_ROOM
    if fits:
        answer = expert_exchange(
            pick_low.reshape(padded, tokens_here).astype(jnp.bfloat16),
            pick_high.reshape(padded, tokens_here).astype(jnp.bfloat16),
            normed_in,
            cotangent,
            joined,
            lowered,
            replicas,
            experts_here,
        )
        returned = answer[:, : width // 2]
        dot_sum = answer[:, width // 2].astype(jnp.float32).reshape(experts_here, TILE, 1)
        weights = [
            jnp.where(pick, gate_window[:, None, :], 0.0)
            .reshape(padded, tokens_here)
            .astype(jnp.bfloat16)
            for pick in (pick_low, pick_high)
        ]
        unit_grad = jnp.concatenate([dot_tn(w, returned) for w in weights], axis=1)
        slot_dot = jnp.sum(jnp.where(pick_low, dot_sum, 0.0), axis=1).T
    else:
        pick = pick_low[:, :CAP].reshape(-1, tokens_here)
        returned, dot_sum = exchange_by_collectives(
            pick.astype(jnp.bfloat16), normed_in, cotangent, w_gate_up, w_down
        )
        weights = jnp.where(pick_low[:, :CAP], gate_window[:, None, :], 0.0)
        unit_grad = dot_tn(weights.reshape(-1, tokens_here).astype(jnp.bfloat16), returned)
        slot_dot = jnp.sum(jnp.where(pick_low[:, :CAP], dot_sum[:, :, None], 0.0), axis=1).T
    gate_grad = jnp.sum(jnp.where(window_hit, slot_dot[:, None, :], 0.0), axis=2)
    chosen_grad = route_scale * (
        gate_grad / affin_sum
        - jnp.sum(gate_grad * chosen, axis=1, keepdims=True) / (affin_sum * affin_sum)
    )
    logit_pick = chosen_grad * chosen * (1.0 - chosen)
    logit_grad = jnp.sum(jnp.where(choose, logit_pick[:, :, None], 0.0), axis=1).astype(
        jnp.bfloat16
    )
    unit_grad = unit_grad + jnp.dot(logit_grad, router, preferred_element_type=jnp.float32)
    scaled = unit_grad * norm_gain
    residual_stream_gradient = (
        cotangent.astype(jnp.float32)
        + inverse * (scaled - normed * jnp.mean(scaled * normed, axis=1, keepdims=True))
    ).astype(jnp.bfloat16)
    hidden_code_gradient = (
        adapter_scale_factor
        * jnp.einsum(
            "td,rd->tr",
            residual_stream_gradient,
            adapter_raise_factor,
            preferred_element_type=jnp.float32,
        )
    ).astype(jnp.bfloat16)
    partial_raise_sum = adapter_scale_factor * jnp.einsum(
        "tr,td->rd", hidden_code, residual_stream_gradient, preferred_element_type=jnp.float32
    )
    part_down = jnp.einsum(
        "tr,th->rh", hidden_code_gradient, heads_out, preferred_element_type=jnp.float32
    )
    mean_down, mean_up = mean_over_devices(
        (part_down, partial_raise_sum), replicas, experts_here
    )
    return (residual_stream_gradient, mean_down, mean_up)


def solution(mesh):
    return jax.shard_map(
        local,
        mesh=mesh,
        in_specs=(
            P(("dp", "expert"), None),
            P(("dp", "expert"), None),
            P(("dp", "expert"), None),
            P(),
            P(),
            P(),
            P(),
            P(("dp", "expert"), None),
            P("expert", None, None, "dp"),
            P("expert", "dp", None),
        ),
        out_specs=(P(("dp", "expert"), None), P(), P()),
        check_vma=False,
    )
```

```python
import functools

import jax
import jax.numpy as jnp
import numpy as np
from jax import lax
from jax.experimental import pallas as pl
from jax.experimental.pallas import tpu as pltpu
from jax.sharding import PartitionSpec as P

ALL_EXP = 256
CAP = 6
TILE = 16
CHUNKS = 7
LANES = 128
VMEM_ROOM = 56 * 1024 * 1024
MESH = pl.DeviceIdType.MESH
F32 = jnp.float32
BF16 = jnp.bfloat16

adapter_scale_factor = 2.0
route_scale = 2.5
norm_eps = 1e-06


def dot_nt(a, b):
    return lax.dot_general(a, b, (((1,), (1,)), ((), ())), preferred_element_type=F32)


def dot_tn(a, b):
    return lax.dot_general(a, b, (((0,), (0,)), ((), ())), preferred_element_type=F32)


def enter(n_dp, n_exp):
    d, e = lax.axis_index("dp"), lax.axis_index("expert")
    barrier = pltpu.get_barrier_semaphore()
    for j in range(1, n_exp):
        pl.semaphore_signal(barrier, inc=1, device_id=(d, e ^ j), device_id_type=MESH)
    for j in range(1, n_dp):
        pl.semaphore_signal(barrier, inc=1, device_id=(d ^ j, e), device_id_type=MESH)
    pl.semaphore_wait(barrier, n_exp + n_dp - 2)
    return d, e


def remote(src, dst, send_sem, recv_sem, device):
    copy = pltpu.make_async_remote_copy(
        src_ref=src,
        dst_ref=dst,
        send_sem=send_sem,
        recv_sem=recv_sem,
        device_id=device,
        device_id_type=MESH,
    )
    copy.start()
    return copy


def expert_kernel(
    n_dp,
    n_exp,
    p_in_ref,
    p_gr_ref,
    q_ref,
    qt_ref,
    nin_ref,
    cot_ref,
    wj_hbm,
    wd_hbm,
    out_ref,
    sent,
    got,
    rows,
    parts,
    arrived,
    back,
    wj,
    wd,
    w_sem,
    a_send,
    a_recv,
    g_send,
    g_recv,
    r_send,
    r_recv,
    b_send,
    b_recv,
):
    width = nin_ref.shape[1]
    slots = n_exp * CAP
    step = width // CHUNKS
    half = width // 2
    piece = half // CHUNKS
    quarter = wd.shape[0]
    load_j = pltpu.make_async_copy(wj_hbm, wj, w_sem.at[0])
    load_d = pltpu.make_async_copy(wd_hbm, wd, w_sem.at[1])
    load_j.start()
    load_d.start()
    d, e = enter(n_dp, n_exp)
    mine = pl.ds(pl.multiple_of(e * TILE, TILE), TILE)

    first = []
    for c in range(CHUNKS):
        cols = pl.ds(c * step, step)
        picked = jnp.dot(p_in_ref[...], nin_ref[:, cols], preferred_element_type=F32)
        picked += jnp.dot(p_gr_ref[...], cot_ref[:, cols], preferred_element_type=F32)
        sent[:, cols] = picked.astype(BF16)
        copies = []
        for j in range(1, n_exp):
            theirs = pl.ds(pl.multiple_of((e ^ j) * TILE, TILE), TILE)
            copies.append(
                remote(
                    sent.at[theirs, cols],
                    got.at[mine, cols],
                    a_send.at[c, j - 1],
                    a_recv.at[c, j - 1],
                    (d, e ^ j),
                )
            )
        got[mine, cols] = sent[mine, cols]
        first.append(copies)

    second, relayed = [], []
    projected = jnp.zeros((n_dp * slots, 2 * quarter), F32)
    hidden_grad = jnp.zeros((n_dp * slots, quarter), F32)
    for c in range(CHUNKS + 2):
        if c < CHUNKS:
            cols = pl.ds(c * step, step)
            for copy in first[c]:
                copy.wait_recv()
            rows[0, :, cols] = jnp.dot(
                q_ref[...], got[:, cols], preferred_element_type=F32
            ).astype(BF16)
            second.append(
                [
                    remote(
                        rows.at[0, :, cols],
                        rows.at[j, :, cols],
                        g_send.at[c, j - 1],
                        g_recv.at[c, j - 1],
                        (d ^ j, e),
                    )
                    for j in (1, 2)
                ]
            )
        if 0 < c <= CHUNKS:
            cols = pl.ds((c - 1) * step, step)
            copies = []
            for j in (1, 2):
                second[c - 1][j - 1].wait_recv()
                some = pl.ds((j - 1) * slots, slots)
                copies.append(
                    remote(
                        rows.at[j, some, cols],
                        rows.at[3, some, cols],
                        g_send.at[c - 1, j + 1],
                        g_recv.at[c - 1, j + 1],
                        (d ^ (3 - j), e),
                    )
                )
            relayed.append(copies)
        if c == 2:
            load_j.wait()
            load_d.wait()
        if c >= 2:
            cols = pl.ds((c - 2) * step, step)
            for copy in relayed[c - 2]:
                copy.wait_recv()
            rows_in = rows[:, :slots, cols].reshape(n_dp * slots, step)
            rows_grad = rows[:, slots:, cols].reshape(n_dp * slots, step)
            projected += jnp.dot(rows_in, wj[cols, :], preferred_element_type=F32)
            hidden_grad += dot_nt(rows_grad, wd[:, cols])
    gate_pre = projected[:, :quarter]
    up_pre = projected[:, quarter:]
    sigma_gate = jax.nn.sigmoid(gate_pre)
    activated = gate_pre * sigma_gate
    hidden = (activated * up_pre).astype(BF16)
    slot_dots = jnp.sum(hidden.astype(F32) * hidden_grad, axis=1, keepdims=True)
    pre_grad = jnp.concatenate(
        [
            hidden_grad * up_pre * sigma_gate * (1.0 + gate_pre * (1.0 - sigma_gate)),
            hidden_grad * activated,
        ],
        axis=1,
    ).astype(BF16)

    spans = [(width, LANES, half, False)]
    spans += [(c * 2 * piece, piece, c * piece, True) for c in range(CHUNKS)]
    count = len(spans)
    third, passed, fourth = [], [], []
    for turn in range(count + 2):
        if turn < count:
            c = turn
            at, size, low, real = spans[c]
            copies = []
            for j in (1, 2) if real else (1,):
                cols = pl.ds(at + (j - 1) * size, size)
                if real:
                    part = dot_nt(pre_grad, wj[pl.ds((j - 1) * half + low, size), :])
                else:
                    part = jnp.broadcast_to(slot_dots, (n_dp * slots, LANES))
                parts[:, :, cols] = part.astype(BF16).reshape(n_dp, slots, size)
                copies.append(
                    [
                        remote(
                            parts.at[block, :, cols],
                            arrived.at[place, :, cols],
                            r_send.at[c, j - 1, place],
                            r_recv.at[c, j - 1, place],
                            (d ^ j, e),
                        )
                        for place, block in ((1, 3), (0, j))
                    ]
                )
            third.append(copies)
        if 0 < turn <= count:
            c = turn - 1
            at, size, low, real = spans[c]
            copies = []
            for j in (1, 2) if real else (1,):
                cols = pl.ds(at + (j - 1) * size, size)
                other = 3 - j
                for copy in third[c][j - 1]:
                    copy.wait_recv()
                both = parts[other, :, cols].astype(F32) + arrived[1, :, cols].astype(F32)
                parts[other, :, cols] = both.astype(BF16)
                copies.append(
                    remote(
                        parts.at[other, :, cols],
                        arrived.at[2, :, cols],
                        r_send.at[c, j - 1, 2],
                        r_recv.at[c, j - 1, 2],
                        (d ^ other, e),
                    )
                )
            passed.append(copies)
        if turn >= 2:
            c = turn - 2
            at, size, low, real = spans[c]
            spread = jnp.zeros((n_exp * TILE, size), F32)
            for j in (1, 2) if real else (1,):
                cols = pl.ds(at + (j - 1) * size, size)
                passed[c][j - 1].wait_recv()
                total = parts[0, :, cols].astype(F32) + arrived[0, :, cols].astype(F32)
                total = (total + arrived[2, :, cols].astype(F32)).astype(BF16)
                spread += jnp.dot(
                    qt_ref[j - 1], total, preferred_element_type=F32
                )
            cols = pl.ds(low, size)
            back[:, cols] = spread.astype(BF16)
            copies = []
            for j in range(1, n_exp):
                theirs = pl.ds(pl.multiple_of((e ^ j) * TILE, TILE), TILE)
                copies.append(
                    remote(
                        back.at[theirs, cols],
                        out_ref.at[mine, cols],
                        b_send.at[c, j - 1],
                        b_recv.at[c, j - 1],
                        (d, e ^ j),
                    )
                )
            out_ref[mine, cols] = back[mine, cols]
            fourth.append(copies)
    for copies in fourth:
        for copy in copies:
            copy.wait_recv()
    third = [sum(copies, []) for copies in third]
    for stage in (first, second, relayed, third, passed, fourth):
        for copies in stage:
            for copy in copies:
                copy.wait_send()


def expert_buffers(n_dp, n_exp, width, quarter):
    slots, padded = n_exp * CAP, n_exp * TILE
    return [
        ((padded, width), BF16),
        ((padded, width), BF16),
        ((n_dp, 2 * slots, width), BF16),
        ((n_dp, slots, width + LANES), BF16),
        ((n_dp - 1, slots, width + LANES), BF16),
        ((padded, width // 2 + LANES), BF16),
        ((width, 2 * quarter), BF16),
        ((quarter, width), BF16),
    ]


def expert_exchange(p_in, p_gr, normed_in, cotangent, joined, lowered, n_dp, n_exp):
    width = normed_in.shape[1]
    quarter = lowered.shape[0]
    slots, padded = n_exp * CAP, n_exp * TILE
    squeeze = np.zeros((2 * slots, padded), np.float32)
    for kind in range(2):
        for e in range(n_exp):
            for s in range(CAP):
                squeeze[kind * slots + e * CAP + s, e * TILE + kind * CAP + s] = 1.0
    vmem = pl.BlockSpec(memory_space=pltpu.VMEM)
    dma = pltpu.SemaphoreType.DMA
    return pl.pallas_call(
        functools.partial(expert_kernel, n_dp, n_exp),
        out_shape=jax.ShapeDtypeStruct((padded, width // 2 + LANES), BF16),
        in_specs=[vmem] * 6 + [pl.BlockSpec(memory_space=pl.ANY)] * 2,
        out_specs=vmem,
        scratch_shapes=[
            pltpu.VMEM(shape, kind)
            for shape, kind in expert_buffers(n_dp, n_exp, width, quarter)
        ]
        + [
            dma((2,)),
            dma((CHUNKS, n_exp - 1)),
            dma((CHUNKS, n_exp - 1)),
            dma((CHUNKS, 4)),
            dma((CHUNKS, 4)),
            dma((CHUNKS + 1, 2, 3)),
            dma((CHUNKS + 1, 2, 3)),
            dma((CHUNKS + 1, n_exp - 1)),
            dma((CHUNKS + 1, n_exp - 1)),
        ],
        compiler_params=pltpu.CompilerParams(
            collective_id=0, has_side_effects=True, vmem_limit_bytes=VMEM_ROOM
        ),
    )(
        p_in,
        p_gr,
        jnp.asarray(squeeze, BF16),
        jnp.asarray(squeeze.reshape(2, slots, padded).transpose(0, 2, 1), BF16),
        normed_in,
        cotangent,
        joined,
        lowered,
    )


def reduce_kernel(n_dp, n_exp, x_ref, o_ref, *scratch):
    d, e = enter(n_dp, n_exp)
    pairs = n_exp // 2
    groups = [
        (2, e & 1, lambda j: (d, e ^ j)),
        (n_dp, d, lambda j: (d ^ j, e)),
        (pairs, e >> 1, lambda j: (d, e ^ (2 * j))),
    ]
    started = []
    held, size, base, bases = x_ref, x_ref.shape[1], 0, []
    for k, (n, index, partner) in enumerate(groups):
        got, total_ref, send, recv = scratch[4 * k : 4 * k + 4]
        size //= n

        def part(i, size=size):
            return pl.ds(pl.multiple_of(i * size, LANES), size)

        copies = [
            remote(
                held.at[:, part(index ^ j)],
                got.at[j - 1],
                send.at[0, j - 1],
                recv.at[0, j - 1],
                partner(j),
            )
            for j in range(1, n)
        ]
        for copy in copies:
            copy.wait_recv()
        started += copies
        total = held[:, part(index)].astype(F32)
        for j in range(1, n):
            total += got[j - 1].astype(F32)
        total_ref[...] = total.astype(BF16)
        held = total_ref
        base = base + index * size
        bases.append((base, size))
    base, size = bases[-1]
    o_ref[:, pl.ds(pl.multiple_of(base, LANES), size)] = held[...]
    for k in reversed(range(3)):
        n, _, partner = groups[k]
        _, _, send, recv = scratch[4 * k : 4 * k + 4]
        base, size = bases[k]
        own = pl.ds(pl.multiple_of(base, LANES), size)
        copies = [
            remote(
                o_ref.at[:, own], o_ref.at[:, own], send.at[1, j - 1], recv.at[1, j - 1], partner(j)
            )
            for j in range(1, n)
        ]
        for copy in copies:
            copy.wait_recv()
        started += copies
    for copy in started:
        copy.wait_send()


def mean_over_devices(terms, n_dp, n_exp):
    rank = terms[0].shape[0]
    total = sum(t.shape[1] for t in terms)
    devices = n_dp * n_exp
    share = -(-total // (devices * LANES)) * LANES
    width = share * devices
    x = jnp.concatenate(
        [t.astype(BF16) for t in terms] + [jnp.zeros((rank, width - total), BF16)], axis=1
    )
    vmem = pl.BlockSpec(memory_space=pltpu.VMEM)
    dma = pltpu.SemaphoreType.DMA
    scratch, size = [], width
    for n in (2, n_dp, n_exp // 2):
        size //= n
        scratch += [pltpu.VMEM((n - 1, rank, size), BF16), pltpu.VMEM((rank, size), BF16)]
        scratch += [dma((2, n - 1)), dma((2, n - 1))]
    out = pl.pallas_call(
        functools.partial(reduce_kernel, n_dp, n_exp),
        out_shape=jax.ShapeDtypeStruct((rank, width), BF16),
        in_specs=[vmem],
        out_specs=vmem,
        scratch_shapes=scratch,
        compiler_params=pltpu.CompilerParams(
            collective_id=1, has_side_effects=True, vmem_limit_bytes=VMEM_ROOM
        ),
    )(x)
    at, outs = 0, []
    for t in terms:
        outs.append(out[:, at : at + t.shape[1]].astype(F32) / devices)
        at += t.shape[1]
    return outs


def expert_rows(rows_in, rows_grad, w_gate_up, w_down):
    quarter = w_down.shape[1]
    width = w_down.shape[2]
    flat_in = rows_in.reshape(-1, width)
    flat_grad = rows_grad.reshape(-1, width)
    joined = w_gate_up.reshape(width, 2 * quarter)
    lowered = w_down.reshape(quarter, width)
    projected = jnp.dot(flat_in, joined, preferred_element_type=jnp.float32)
    gate_pre = projected[:, :quarter]
    up_pre = projected[:, quarter:]
    sigma_gate = jax.nn.sigmoid(gate_pre)
    activated = gate_pre * sigma_gate
    hidden = (activated * up_pre).astype(jnp.bfloat16)
    hidden_grad = jnp.einsum("md,hd->mh", flat_grad, lowered, preferred_element_type=jnp.float32)
    slot_dots = jnp.sum(hidden.astype(jnp.float32) * hidden_grad, axis=1)
    pre_grad = jnp.concatenate(
        [
            hidden_grad * up_pre * sigma_gate * (1.0 + gate_pre * (1.0 - sigma_gate)),
            hidden_grad * activated,
        ],
        axis=1,
    ).astype(jnp.bfloat16)
    partial_rows = jnp.einsum("mk,dk->md", pre_grad, joined, preferred_element_type=jnp.float32)
    return (partial_rows, slot_dots)


def exchange_by_collectives(pick, normed_in, cotangent, w_gate_up, w_down):
    width = normed_in.shape[1]
    experts_here, replicas = lax.axis_size("expert"), lax.axis_size("dp")
    gathered = []
    for rows in (normed_in, cotangent):
        send = jnp.dot(pick, rows, preferred_element_type=F32).astype(BF16)
        got = lax.all_to_all(
            send.reshape(experts_here, CAP, width), "expert", 0, 0, tiled=True
        )
        gathered.append(lax.all_gather(got, "dp", axis=0, tiled=True))
    partial_rows, slot_dots = expert_rows(*gathered, w_gate_up, w_down)
    sums = []
    for part in (partial_rows, slot_dots[:, None]):
        part = part.astype(BF16).reshape(replicas * experts_here, CAP, -1)
        part = lax.psum_scatter(part, "dp", scatter_dimension=0, tiled=True)
        part = lax.all_to_all(part.astype(BF16), "expert", 0, 0, tiled=True)
        sums.append(part)
    return sums[0].reshape(experts_here * CAP, width), sums[1][:, :, 0].astype(F32)


def local(
    stream,
    heads_out,
    cotangent,
    adapter_down,
    adapter_raise_factor,
    norm_gain,
    router,
    expert_ids,
    w_gate_up,
    w_down,
):
    tokens_here = stream.shape[0]
    width = stream.shape[1]
    experts_here = lax.axis_size("expert")
    replicas = lax.axis_size("dp")
    hidden_code = jnp.einsum(
        "th,rh->tr", heads_out, adapter_down, preferred_element_type=jnp.float32
    ).astype(jnp.bfloat16)
    combined_result = stream.astype(jnp.float32) + adapter_scale_factor * jnp.dot(
        hidden_code, adapter_raise_factor, preferred_element_type=jnp.float32
    )
    inverse = lax.rsqrt(
        jnp.mean(combined_result * combined_result, axis=1, keepdims=True) + norm_eps
    )
    normed = combined_result * inverse
    normed_in = (normed * norm_gain).astype(jnp.bfloat16)
    logits = jnp.einsum("td,ed->te", normed_in, router, preferred_element_type=jnp.float32)
    affinity = jax.nn.sigmoid(logits)
    choose = expert_ids[:, :, None] == jnp.arange(ALL_EXP, dtype=jnp.int32)[None, None, :]
    chosen = jnp.sum(jnp.where(choose, affinity[:, None, :], 0.0), axis=2)
    affin_sum = jnp.sum(chosen, axis=1, keepdims=True)
    gate_weights = route_scale * chosen / affin_sum
    window = jnp.arange(experts_here, dtype=jnp.int32)
    window_hit = expert_ids[:, :, None] == window[None, None, :]
    hit_any = jnp.sum(window_hit.astype(jnp.int32), axis=1).T
    gate_window = jnp.sum(jnp.where(window_hit, gate_weights[:, :, None], 0.0), axis=1).T
    token = jnp.arange(tokens_here, dtype=jnp.int32)
    earlier = (token[:, None] < token[None, :]).astype(jnp.bfloat16)
    before = jnp.dot(
        hit_any.astype(jnp.bfloat16), earlier, preferred_element_type=jnp.float32
    ).astype(jnp.int32)
    position = jnp.where(hit_any == 1, before, -ALL_EXP)
    slot = jnp.arange(TILE, dtype=jnp.int32)[None, :, None]
    pick_low = position[:, None, :] == slot
    pick_high = position[:, None, :] == slot - CAP
    padded = experts_here * TILE
    joined = w_gate_up.reshape(width, -1)
    lowered = w_down.reshape(-1, width)
    buffers = expert_buffers(replicas, experts_here, width, lowered.shape[0])
    fits = replicas == 4 and sum(int(np.prod(shape)) * 2 for shape, _ in buffers) < 0.75 * VMEM_ROOM
    if fits:
        answer = expert_exchange(
            pick_low.reshape(padded, tokens_here).astype(jnp.bfloat16),
            pick_high.reshape(padded, tokens_here).astype(jnp.bfloat16),
            normed_in,
            cotangent,
            joined,
            lowered,
            replicas,
            experts_here,
        )
        returned = answer[:, : width // 2]
        dot_sum = answer[:, width // 2].astype(jnp.float32).reshape(experts_here, TILE, 1)
        weights = [
            jnp.where(pick, gate_window[:, None, :], 0.0)
            .reshape(padded, tokens_here)
            .astype(jnp.bfloat16)
            for pick in (pick_low, pick_high)
        ]
        unit_grad = jnp.concatenate([dot_tn(w, returned) for w in weights], axis=1)
        slot_dot = jnp.sum(jnp.where(pick_low, dot_sum, 0.0), axis=1).T
    else:
        pick = pick_low[:, :CAP].reshape(-1, tokens_here)
        returned, dot_sum = exchange_by_collectives(
            pick.astype(jnp.bfloat16), normed_in, cotangent, w_gate_up, w_down
        )
        weights = jnp.where(pick_low[:, :CAP], gate_window[:, None, :], 0.0)
        unit_grad = dot_tn(weights.reshape(-1, tokens_here).astype(jnp.bfloat16), returned)
        slot_dot = jnp.sum(jnp.where(pick_low[:, :CAP], dot_sum[:, :, None], 0.0), axis=1).T
    gate_grad = jnp.sum(jnp.where(window_hit, slot_dot[:, None, :], 0.0), axis=2)
    chosen_grad = route_scale * (
        gate_grad / affin_sum
        - jnp.sum(gate_grad * chosen, axis=1, keepdims=True) / (affin_sum * affin_sum)
    )
    logit_pick = chosen_grad * chosen * (1.0 - chosen)
    logit_grad = jnp.sum(jnp.where(choose, logit_pick[:, :, None], 0.0), axis=1).astype(
        jnp.bfloat16
    )
    unit_grad = unit_grad + jnp.dot(logit_grad, router, preferred_element_type=jnp.float32)
    scaled = unit_grad * norm_gain
    residual_stream_gradient = (
        cotangent.astype(jnp.float32)
        + inverse * (scaled - normed * jnp.mean(scaled * normed, axis=1, keepdims=True))
    ).astype(jnp.bfloat16)
    hidden_code_gradient = (
        adapter_scale_factor
        * jnp.einsum(
            "td,rd->tr",
            residual_stream_gradient,
            adapter_raise_factor,
            preferred_element_type=jnp.float32,
        )
    ).astype(jnp.bfloat16)
    partial_raise_sum = adapter_scale_factor * jnp.einsum(
        "tr,td->rd", hidden_code, residual_stream_gradient, preferred_element_type=jnp.float32
    )
    part_down = jnp.einsum(
        "tr,th->rh", hidden_code_gradient, heads_out, preferred_element_type=jnp.float32
    )
    mean_down, mean_up = mean_over_devices(
        (part_down, partial_raise_sum), replicas, experts_here
    )
    return (residual_stream_gradient, mean_down, mean_up)


def solution(mesh):
    return jax.shard_map(
        local,
        mesh=mesh,
        in_specs=(
            P(("dp", "expert"), None),
            P(("dp", "expert"), None),
            P(("dp", "expert"), None),
            P(),
            P(),
            P(),
            P(),
            P(("dp", "expert"), None),
            P("expert", None, None, "dp"),
            P("expert", "dp", None),
        ),
        out_specs=(P(("dp", "expert"), None), P(), P()),
        check_vma=False,
    )
```
